32 devices in a mesh: dp: 2 (over y), expert: 16 (over z, x, core).
Axes of the slice: x: 2, y: 2, z: 4, core: 2. Of those that a mesh axis runs over, the one named last changes fastest.
Arguments:
- tokens: bfloat16 [768, 4096], P(('dp', 'expert')), may hold values from -6 to 6
- out_grad: bfloat16 [768, 4096], P(('dp', 'expert')), may hold values from -6 to 6
- routes: int32 [768, 8], P(('dp', 'expert')), may hold values from 0 to 15, all different within a row; in each aligned block of 24 rows (0 to 23, 24 to 47, ...) at most 18 rows name the same one
- gates: bfloat16 [768, 8], P(('dp', 'expert')), may hold values from 0.099609375 to 0.5
- w_gate: bfloat16 [16, 768, 4096], P('expert', 'dp'), may hold values from -0.09375 to 0.09375
- w_up: bfloat16 [16, 768, 4096], P('expert', 'dp'), may hold values from -0.09375 to 0.09375
- w_down: bfloat16 [16, 768, 4096], P('expert', 'dp'), may hold values from -0.21875 to 0.21875
Outputs:
- d_tokens: bfloat16 [768, 4096], P(('dp', 'expert'))
- d_gate: bfloat16 [16, 768, 4096], P('expert', 'dp')
- d_up: bfloat16 [16, 768, 4096], P('expert', 'dp')
- d_down: bfloat16 [16, 768, 4096], P('expert', 'dp')
The draws below stay inside these ranges and needn't reach their ends.
Inputs may be any that keep to these rules, and one draw needn't show every extreme that they name: `routes`: each row names 8 different experts. Within the 24 rows of one device no expert is named by more than 18 rows, and in every draw some expert is named by exactly 18 rows of some device.
All inputs are finite; a program needn't handle non-finite values.
Results may differ from the reference program's by a relative error of at most 0.015.
Values may be sent and summed in bfloat16 or wider, within the bound.
No kernel may reach another device: no remote copies, remote signals or barrier semaphores. Data moves between devices by JAX's collectives and lax.ppermute only.
A program may use at most 128 MiB of HBM per device.

```python
import math
import jax
import jax.numpy as jnp
import numpy as np
from jax import lax

D = 4096
HIDDEN_SIZE = 768
TOP_K = 8
TOK_DEV = 24
EXPERTS = 16
CAP = 18
TOKENS = 768
N_DP = 2


def level_of(own_key, extent, split, least, largest):
    def one(axis_at, blocks):
        steps = jax.random.uniform(jax.random.fold_in(jax.random.fold_in(own_key, 6), axis_at), (blocks,), jnp.float32, least / len(split), largest / len(split))
        return jnp.repeat(jnp.exp(steps), extent[axis_at] // blocks).reshape((-1,) + (1,) * (len(extent) - axis_at - 1))

    gain = one(*split[0])
    for cut in split[1:]:
        gain = gain * one(*cut)
    return gain


def shared_out(rng, own, number, rows, number_of, top, most, slope):
    order = jax.random.permutation(rng, number_of)
    crowded, ordinary = shares(number_of, rows * top, most, slope, True), shares(number_of, rows * top, most, slope, False)
    places = jnp.arange(number_of)

    def named(lengths, rotation):
        used = int((lengths > 0).sum())
        fixed = max(1, used // 4)
        moved = fixed + (places - fixed + rotation * (used - fixed)) % max(1, number_of - fixed)
        return jnp.zeros((number_of,), jnp.int32).at[order[jnp.where(places < fixed, places, moved)]].set(jnp.asarray(lengths, jnp.int32))

    lengths = jnp.where(number % 4 == 0, named(crowded, number // 4), named(ordinary, number - number // 4 - 1))
    mixed = jax.random.permutation(jax.random.fold_in(own, 3), number_of)
    donor, taker = mixed[0:number_of // 2 * 2:2], mixed[1:number_of // 2 * 2:2]
    slack = jnp.minimum(lengths[donor] - 1, most - lengths[taker]) // 2
    slack = jnp.where((donor == order[0]) | (taker == order[0]) | (lengths[taker] == 0), 0, jnp.maximum(slack, 0))
    moved = jax.random.randint(jax.random.fold_in(own, 4), (number_of // 2,), 0, 1 << 20) % (slack + 1)
    lengths = lengths.at[donor].add(-moved).at[taker].add(moved)
    items = jnp.searchsorted(jnp.cumsum(lengths), jnp.arange(rows * top), side="right").astype(jnp.int32)
    table = items.reshape(top, rows).T
    table = table[jax.random.permutation(jax.random.fold_in(own, 1), rows)]
    rotation = jax.random.randint(jax.random.fold_in(own, 2), (rows, 1), 0, top)
    return jnp.take_along_axis(table, (jnp.arange(top)[None, :] + rotation) % top, axis=1)


def shares(number_of, total, bound, lean, full):
    portions = [(1 << 20) // math.isqrt(standing ** lean) + 1 for standing in range(1, number_of + 1)]
    largest = bound if full else min(bound, max(-(-total // number_of), total * portions[0] // sum(portions)))
    least = 1 if total - largest >= number_of - 1 else 0
    holding, rest = [largest] + [least] * (number_of - 1), total - largest - least * (number_of - 1)
    while rest > 0:
        movable = [i for i in range(1, number_of) if holding[i] < largest] or [i for i in range(1, number_of) if holding[i] < bound]
        pool, left = sum([portions[i] for i in movable]), rest
        for i in movable:
            addition = min(bound - holding[i], max(1, left * portions[i] // pool), rest)
            holding[i] = holding[i] + addition
            rest = rest - addition
    return np.array(holding)


def bell_draw(own_key, shape, scale, limit, pieces=(), kind=jnp.bfloat16):
    drawn = jax.random.normal(own_key, shape, jnp.float32) * scale
    if len(pieces) > 0:
        drawn = level_of(own_key, shape, pieces, -0.22, 0.18) * drawn
    return jnp.clip(drawn, min=-limit, max=limit).astype(kind)


def setup_inputs(seed: int = 0) -> dict:
    key_list = jax.random.split(jax.random.key(seed), 8)
    tokens = bell_draw(key_list[0], (TOKENS, D), 1.0, 6.0, ((0, 32),))
    out_grad = bell_draw(key_list[1], (TOKENS, D), 1.0, 6.0, ((0, 32),))
    routes_keys = jax.random.split(jax.random.fold_in(key_list[2], 1), TOKENS // TOK_DEV)
    routes_turns = jax.random.permutation(jax.random.fold_in(key_list[2], 3), TOKENS // TOK_DEV)
    routes = jax.vmap(lambda own, number: shared_out(jax.random.fold_in(key_list[2], 2), own, number, TOK_DEV, EXPERTS, TOP_K, CAP, 2))(routes_keys, routes_turns).reshape((TOKENS, TOP_K))
    gates = jnp.clip(0.099609375 + 0.40039062 * jax.random.uniform(key_list[3], (TOKENS, TOP_K), jnp.float32) ** level_of(key_list[3], (TOKENS, TOP_K), ((0, 32),), -0.2, 0.2), 0.099609375, 0.5).astype(jnp.bfloat16)
    w_gate = bell_draw(key_list[4], (EXPERTS, HIDDEN_SIZE, D), D ** -0.5, 0.09375, ((0, 16), (1, 2)))
    w_up = bell_draw(key_list[5], (EXPERTS, HIDDEN_SIZE, D), D ** -0.5, 0.09375, ((0, 16), (1, 2)))
    w_down = bell_draw(key_list[6], (EXPERTS, HIDDEN_SIZE, D), HIDDEN_SIZE ** -0.5, 0.21875, ((0, 16), (1, 2)))
    return {"tokens": tokens, "out_grad": out_grad, "routes": routes, "gates": gates, "w_gate": w_gate, "w_up": w_up, "w_down": w_down}


def reference(tokens, out_grad, routes, gates, w_gate, w_up, w_down):
    blocks = TOKENS // TOK_DEV
    quarter = HIDDEN_SIZE // N_DP
    expert_ids = jnp.arange(EXPERTS, dtype=jnp.int32)
    onehot = (routes[:, :, None] == expert_ids).astype(jnp.int32)
    chosen = jnp.sum(onehot, axis=1).astype(jnp.int32).reshape(blocks, TOK_DEV, EXPERTS)
    earlier = (jnp.cumsum(chosen, axis=1).astype(jnp.int32) - chosen).reshape(TOKENS, EXPERTS)
    slot_index = jnp.sum(onehot * earlier[:, None, :], axis=2).astype(jnp.int32)
    source = (jnp.arange(TOKENS, dtype=jnp.int32) // TOK_DEV).astype(jnp.int32)
    place_col = (source[:, None] * CAP + slot_index).astype(jnp.int32)
    pair_ids = jnp.arange(TOKENS * TOP_K, dtype=jnp.int32).reshape(TOKENS, TOP_K)
    table = jnp.full((EXPERTS, blocks * CAP), TOKENS * TOP_K, jnp.int32)
    table = table.at[routes, place_col].set(pair_ids)
    input_ext = jnp.concatenate([tokens, jnp.zeros((1, D), tokens.dtype)], axis=0)
    grad_ext = jnp.concatenate([out_grad, jnp.zeros((1, D), out_grad.dtype)], axis=0)
    gate_ext = jnp.concatenate([gates.reshape(-1).astype(jnp.float32), jnp.zeros((1,), jnp.float32)])

    def expert_step(dx_acc, inputs):
        pair_row, gate_w, up_w, down_w = inputs
        token_row = (pair_row // TOP_K).astype(jnp.int32)
        x_slot = input_ext[token_row]
        g_slot = (gate_ext[pair_row][:, None] * grad_ext[token_row].astype(jnp.float32)).astype(jnp.bfloat16)
        gate_pre = jnp.dot(x_slot, gate_w.T, preferred_element_type=jnp.float32)
        up_pre = jnp.dot(x_slot, up_w.T, preferred_element_type=jnp.float32)
        sigmoid_gate = jax.nn.sigmoid(gate_pre)
        silu_gate = gate_pre * sigmoid_gate
        hidden = (silu_gate * up_pre).astype(jnp.bfloat16)
        d_hidden = jnp.dot(g_slot, down_w.T, preferred_element_type=jnp.float32)
        d_up_act = (d_hidden * silu_gate).astype(jnp.bfloat16)
        d_gate_act = (d_hidden * up_pre * sigmoid_gate * (1.0 + gate_pre * (1.0 - sigmoid_gate))).astype(jnp.bfloat16)
        grad_down = jnp.dot(hidden.T, g_slot, preferred_element_type=jnp.float32).astype(jnp.bfloat16)
        grad_gate = jnp.dot(d_gate_act.T, x_slot, preferred_element_type=jnp.float32).astype(jnp.bfloat16)
        grad_up = jnp.dot(d_up_act.T, x_slot, preferred_element_type=jnp.float32).astype(jnp.bfloat16)
        rows_count = x_slot.shape[0]
        gate_parts = jnp.einsum("rqf,qfd->qrd", d_gate_act.astype(jnp.float32).reshape(rows_count, N_DP, quarter), gate_w.astype(jnp.float32).reshape(N_DP, quarter, D))
        up_parts = jnp.einsum("rqf,qfd->qrd", d_up_act.astype(jnp.float32).reshape(rows_count, N_DP, quarter), up_w.astype(jnp.float32).reshape(N_DP, quarter, D))
        rounded = lax.optimization_barrier((gate_parts + up_parts).astype(jnp.bfloat16))
        dx_slot = jnp.sum(rounded.astype(jnp.float32), axis=0)
        dx_acc = dx_acc.at[token_row].add(dx_slot)
        return dx_acc, (grad_gate, grad_up, grad_down)

    start = jnp.zeros((TOKENS + 1, D), jnp.float32)
    dx_acc, grads = lax.scan(expert_step, start, (table, w_gate, w_up, w_down))
    return dx_acc[:TOKENS].astype(jnp.bfloat16), grads[0], grads[1], grads[2]
```

```python
from functools import partial

import jax
import jax.numpy as jnp
from jax import lax
from jax.sharding import PartitionSpec as P


def cell_match(routes, experts, capacity):
    expert_ids = jnp.arange(experts, dtype=jnp.int32)
    onehot = (routes[:, :, None] == expert_ids).astype(jnp.int32)
    chosen = jnp.sum(onehot, axis=1)
    earlier = jnp.cumsum(chosen, axis=0) - chosen
    slot_index = jnp.sum(onehot * earlier[:, None, :], axis=2)
    target = routes * capacity + slot_index
    cell_ids = jnp.arange(experts * capacity, dtype=jnp.int32)
    return target[:, :, None] == cell_ids


def placement(matches, experts, capacity):
    return jnp.any(matches, axis=1).reshape(-1, experts, capacity).astype(jnp.bfloat16)


def weighting(matches, gates, experts, capacity):
    spread = jnp.where(matches, gates.astype(jnp.float32)[:, :, None], 0.0)
    return jnp.sum(spread, axis=1).reshape(-1, experts, capacity)


def slot_plan(tokens, out_grad, routes, gates, w_gate, w_up, w_down):
    tok_rows, features = tokens.shape
    top_count = routes.shape[1]
    experts = lax.axis_size("expert")
    groups = lax.axis_size("dp")
    capacity = max(2, min(tok_rows, 3 * tok_rows * top_count // (2 * experts)))
    match_fn = partial(cell_match, experts=experts, capacity=capacity)
    place_fn = partial(placement, experts=experts, capacity=capacity)
    weight_fn = partial(weighting, experts=experts, capacity=capacity)
    own_match = match_fn(routes)
    own_place = place_fn(own_match)
    own_weight = weight_fn(own_match, gates)
    input_send = jnp.einsum(
        "tec,td->ecd", own_place, tokens, preferred_element_type=jnp.float32
    ).astype(jnp.bfloat16)
    grad_send = jnp.einsum(
        "tec,td->ecd", own_weight, out_grad.astype(jnp.float32), precision=lax.Precision.HIGHEST
    ).astype(jnp.bfloat16)
    input_recv, grad_recv = (
        lax.all_to_all(input_send, "expert", split_axis=0, concat_axis=0, tiled=True),
        lax.all_to_all(grad_send, "expert", split_axis=0, concat_axis=0, tiled=True),
    )
    input_recv = input_recv.reshape(experts, 1, capacity, features)
    grad_recv = grad_recv.reshape(experts, 1, capacity, features)
    input_slots, grad_slots = (
        lax.all_gather(input_recv, "dp", axis=1, tiled=True),
        lax.all_gather(grad_recv, "dp", axis=1, tiled=True),
    )
    input_rows = input_slots.reshape(-1, features)
    grad_rows = grad_slots.reshape(-1, features)
    gate_w = w_gate[0]
    up_w = w_up[0]
    down_w = w_down[0]
    gate_pre = jnp.einsum("rd,fd->rf", input_rows, gate_w, preferred_element_type=jnp.float32)
    up_pre = jnp.einsum("rd,fd->rf", input_rows, up_w, preferred_element_type=jnp.float32)
    sigmoid_gate = jax.nn.sigmoid(gate_pre)
    silu_gate = gate_pre * sigmoid_gate
    hidden = (silu_gate * up_pre).astype(jnp.bfloat16)
    d_hidden = jnp.einsum("rd,fd->rf", grad_rows, down_w, preferred_element_type=jnp.float32)
    d_up_act = (d_hidden * silu_gate).astype(jnp.bfloat16)
    d_gate_act = (
        d_hidden * up_pre * sigmoid_gate * (1.0 + gate_pre * (1.0 - sigmoid_gate))
    ).astype(jnp.bfloat16)
    grad_down = jnp.einsum(
        "rf,rd->fd", hidden, grad_rows, preferred_element_type=jnp.float32
    ).astype(jnp.bfloat16)
    grad_gate = jnp.einsum(
        "rf,rd->fd", d_gate_act, input_rows, preferred_element_type=jnp.float32
    ).astype(jnp.bfloat16)
    grad_up = jnp.einsum(
        "rf,rd->fd", d_up_act, input_rows, preferred_element_type=jnp.float32
    ).astype(jnp.bfloat16)
    partial_sum = jnp.einsum("rf,fd->rd", d_gate_act, gate_w, preferred_element_type=jnp.float32)
    partial_sum = partial_sum + jnp.einsum(
        "rf,fd->rd", d_up_act, up_w, preferred_element_type=jnp.float32
    )
    rounded = partial_sum.astype(jnp.bfloat16).reshape(experts, groups, capacity, features)
    held = lax.optimization_barrier(rounded).astype(jnp.float32)
    slot_total = lax.psum_scatter(
        held.astype(jnp.bfloat16), "dp", scatter_dimension=1, tiled=True
    ).astype(jnp.float32)
    returned = lax.all_to_all(
        slot_total[:, 0].astype(jnp.bfloat16), "expert", split_axis=0, concat_axis=0, tiled=True
    ).astype(jnp.float32)
    summed = jnp.einsum(
        "tec,ecd->td", own_place.astype(jnp.float32), returned, precision=lax.Precision.HIGHEST
    )
    return (summed.astype(jnp.bfloat16), grad_gate[None], grad_up[None], grad_down[None])


def swapped(x, axis, bits):
    count = lax.axis_size(axis)
    return lax.ppermute(x, axis, [(i, i ^ bits) for i in range(count)])


def gate_of_expert(routes, gates, experts):
    hit = routes[:, :, None] == jnp.arange(experts, dtype=jnp.int32)
    return jnp.sum(jnp.where(hit, gates[:, :, None], 0), axis=1).astype(jnp.bfloat16)


def dense_plan(tokens, out_grad, routes, gates, w_gate, w_up, w_down):
    rows, features = tokens.shape
    half = features // 2
    experts = lax.axis_size("expert")
    layers = experts // 4
    over_core = partial(swapped, axis="expert", bits=1)
    over_x = partial(swapped, axis="expert", bits=2)
    over_y = partial(swapped, axis="dp", bits=1)

    def over_z(x, step):
        return swapped(x, "expert", 4 * step) if step else x

    def summed(x, y):
        return (x.astype(jnp.float32) + y.astype(jnp.float32)).astype(jnp.bfloat16)

    scales = gate_of_expert(routes, gates, experts)[None]
    for move in (over_core, over_x, over_y):
        scales = jnp.concatenate([scales, move(scales)])
    scales = jnp.stack([over_z(scales, step) for step in range(layers)])
    own = jnp.arange(experts, dtype=jnp.int32) == lax.axis_index("expert")
    scales = jnp.sum(jnp.where(own, scales.astype(jnp.float32), 0.0), axis=-1)
    scales = scales.reshape(layers, -1, 1)

    gate_w = w_gate[0]
    up_w = w_up[0]
    down_w = w_down[0]
    mine = jnp.stack([tokens, out_grad])
    inputs, grads, hiddens, gate_acts, up_acts = [], [], [], [], []
    total = None
    for step in range(layers):
        here = over_z(mine, step)
        from_x = over_x(here)
        from_y = over_y(here)
        from_xy = jnp.concatenate(
            [over_x(from_y[:, :, :half]), over_y(from_x[:, :, half:])], axis=2
        )
        lane = jnp.stack([here, from_x, from_y, from_xy], axis=1)
        both = jnp.stack([lane, over_core(lane)], axis=2)
        both = both.reshape(2, -1, features)
        x_rows, g_rows = both[0], both[1]
        scale = scales[step]
        gate_pre = jnp.einsum("rd,fd->rf", x_rows, gate_w, preferred_element_type=jnp.float32)
        up_pre = jnp.einsum("rd,fd->rf", x_rows, up_w, preferred_element_type=jnp.float32)
        d_hidden = scale * jnp.einsum("rd,fd->rf", g_rows, down_w, preferred_element_type=jnp.float32)
        sigmoid_gate = jax.nn.sigmoid(gate_pre)
        silu_gate = gate_pre * sigmoid_gate
        hidden = (scale * silu_gate * up_pre).astype(jnp.bfloat16)
        d_up_act = (d_hidden * silu_gate).astype(jnp.bfloat16)
        d_gate_act = (
            d_hidden * up_pre * sigmoid_gate * (1.0 + gate_pre * (1.0 - sigmoid_gate))
        ).astype(jnp.bfloat16)
        part = jnp.einsum("rf,fd->rd", d_gate_act, gate_w, preferred_element_type=jnp.float32)
        part = part + jnp.einsum("rf,fd->rd", d_up_act, up_w, preferred_element_type=jnp.float32)
        part = part.astype(jnp.bfloat16).reshape(4, 2, rows, features)
        lane_sum = summed(part[:, 0], over_core(part[:, 1]))
        left, right = lane_sum[:, :, :half], lane_sum[:, :, half:]
        left = summed(left[0::2], over_x(left[1::2]))
        right = summed(right[:2], over_y(right[2:]))
        left = summed(left[0], over_y(left[1]))
        right = summed(right[0], over_x(right[1]))
        back = over_z(jnp.concatenate([left, right], axis=1), step).astype(jnp.float32)
        total = back if total is None else total + back
        inputs.append(x_rows)
        grads.append(g_rows)
        hiddens.append(hidden)
        gate_acts.append(d_gate_act)
        up_acts.append(d_up_act)

    def weight_grad(acts, sides):
        return jnp.einsum(
            "rf,rd->fd", acts, sides, preferred_element_type=jnp.float32
        ).astype(jnp.bfloat16)[None]

    all_inputs = jnp.concatenate(inputs)
    return (
        total.astype(jnp.bfloat16),
        weight_grad(jnp.concatenate(gate_acts), all_inputs),
        weight_grad(jnp.concatenate(up_acts), all_inputs),
        weight_grad(jnp.concatenate(hiddens), jnp.concatenate(grads)),
    )


def per_device(tokens, out_grad, routes, gates, w_gate, w_up, w_down):
    tok_rows, top_count = routes.shape
    experts = lax.axis_size("expert")
    capacity = max(2, min(tok_rows, 3 * tok_rows * top_count // (2 * experts)))
    crowded = 2 * capacity >= tok_rows and lax.axis_size("dp") == 2 and experts in (4, 8, 16)
    plan = dense_plan if crowded else slot_plan
    return plan(tokens, out_grad, routes, gates, w_gate, w_up, w_down)


def solution(mesh):
    in_specs = (
        P(("dp", "expert"), None),
        P(("dp", "expert"), None),
        P(("dp", "expert"), None),
        P(("dp", "expert"), None),
        P("expert", "dp", None),
        P("expert", "dp", None),
        P("expert", "dp", None),
    )
    out_specs = (
        P(("dp", "expert"), None),
        P("expert", "dp", None),
        P("expert", "dp", None),
        P("expert", "dp", None),
    )
    return jax.shard_map(
        per_device, mesh=mesh, in_specs=in_specs, out_specs=out_specs, check_vma=False
    )
```

```python
from functools import partial

import jax
import jax.numpy as jnp
from jax import lax
from jax.sharding import PartitionSpec as P


def cell_match(routes, experts, capacity):
    expert_ids = jnp.arange(experts, dtype=jnp.int32)
    onehot = (routes[:, :, None] == expert_ids).astype(jnp.int32)
    chosen = jnp.sum(onehot, axis=1)
    earlier = jnp.cumsum(chosen, axis=0) - chosen
    slot_index = jnp.sum(onehot * earlier[:, None, :], axis=2)
    target = routes * capacity + slot_index
    cell_ids = jnp.arange(experts * capacity, dtype=jnp.int32)
    return target[:, :, None] == cell_ids


def placement(matches, experts, capacity):
    return jnp.any(matches, axis=1).reshape(-1, experts, capacity).astype(jnp.bfloat16)


def weighting(matches, gates, experts, capacity):
    spread = jnp.where(matches, gates.astype(jnp.float32)[:, :, None], 0.0)
    return jnp.sum(spread, axis=1).reshape(-1, experts, capacity)


def slot_plan(tokens, out_grad, routes, gates, w_gate, w_up, w_down):
    tok_rows, features = tokens.shape
    top_count = routes.shape[1]
    experts = lax.axis_size("expert")
    groups = lax.axis_size("dp")
    capacity = max(2, min(tok_rows, 3 * tok_rows * top_count // (2 * experts)))
    match_fn = partial(cell_match, experts=experts, capacity=capacity)
    place_fn = partial(placement, experts=experts, capacity=capacity)
    weight_fn = partial(weighting, experts=experts, capacity=capacity)
    own_match = match_fn(routes)
    own_place = place_fn(own_match)
    own_weight = weight_fn(own_match, gates)
    input_send = jnp.einsum(
        "tec,td->ecd", own_place, tokens, preferred_element_type=jnp.float32
    ).astype(jnp.bfloat16)
    grad_send = jnp.einsum(
        "tec,td->ecd", own_weight, out_grad.astype(jnp.float32), precision=lax.Precision.HIGHEST
    ).astype(jnp.bfloat16)
    input_recv, grad_recv = (
        lax.all_to_all(input_send, "expert", split_axis=0, concat_axis=0, tiled=True),
        lax.all_to_all(grad_send, "expert", split_axis=0, concat_axis=0, tiled=True),
    )
    input_recv = input_recv.reshape(experts, 1, capacity, features)
    grad_recv = grad_recv.reshape(experts, 1, capacity, features)
    input_slots, grad_slots = (
        lax.all_gather(input_recv, "dp", axis=1, tiled=True),
        lax.all_gather(grad_recv, "dp", axis=1, tiled=True),
    )
    input_rows = input_slots.reshape(-1, features)
    grad_rows = grad_slots.reshape(-1, features)
    gate_w = w_gate[0]
    up_w = w_up[0]
    down_w = w_down[0]
    gate_pre = jnp.einsum("rd,fd->rf", input_rows, gate_w, preferred_element_type=jnp.float32)
    up_pre = jnp.einsum("rd,fd->rf", input_rows, up_w, preferred_element_type=jnp.float32)
    sigmoid_gate = jax.nn.sigmoid(gate_pre)
    silu_gate = gate_pre * sigmoid_gate
    hidden = (silu_gate * up_pre).astype(jnp.bfloat16)
    d_hidden = jnp.einsum("rd,fd->rf", grad_rows, down_w, preferred_element_type=jnp.float32)
    d_up_act = (d_hidden * silu_gate).astype(jnp.bfloat16)
    d_gate_act = (
        d_hidden * up_pre * sigmoid_gate * (1.0 + gate_pre * (1.0 - sigmoid_gate))
    ).astype(jnp.bfloat16)
    grad_down = jnp.einsum(
        "rf,rd->fd", hidden, grad_rows, preferred_element_type=jnp.float32
    ).astype(jnp.bfloat16)
    grad_gate = jnp.einsum(
        "rf,rd->fd", d_gate_act, input_rows, preferred_element_type=jnp.float32
    ).astype(jnp.bfloat16)
    grad_up = jnp.einsum(
        "rf,rd->fd", d_up_act, input_rows, preferred_element_type=jnp.float32
    ).astype(jnp.bfloat16)
    partial_sum = jnp.einsum("rf,fd->rd", d_gate_act, gate_w, preferred_element_type=jnp.float32)
    partial_sum = partial_sum + jnp.einsum(
        "rf,fd->rd", d_up_act, up_w, preferred_element_type=jnp.float32
    )
    rounded = partial_sum.astype(jnp.bfloat16).reshape(experts, groups, capacity, features)
    held = lax.optimization_barrier(rounded).astype(jnp.float32)
    slot_total = lax.psum_scatter(
        held.astype(jnp.bfloat16), "dp", scatter_dimension=1, tiled=True
    ).astype(jnp.float32)
    returned = lax.all_to_all(
        slot_total[:, 0].astype(jnp.bfloat16), "expert", split_axis=0, concat_axis=0, tiled=True
    ).astype(jnp.float32)
    summed = jnp.einsum(
        "tec,ecd->td", own_place.astype(jnp.float32), returned, precision=lax.Precision.HIGHEST
    )
    return (summed.astype(jnp.bfloat16), grad_gate[None], grad_up[None], grad_down[None])


def swapped(x, axis, bits):
    count = lax.axis_size(axis)
    return lax.ppermute(x, axis, [(i, i ^ bits) for i in range(count)])


over_core = partial(swapped, axis="expert", bits=1)
over_x = partial(swapped, axis="expert", bits=2)
over_z = partial(swapped, axis="expert", bits=4)
over_far_z = partial(swapped, axis="expert", bits=8)
over_y = partial(swapped, axis="dp", bits=1)
together = lax.optimization_barrier
LANES = 128


def gate_of_expert(routes, gates, experts):
    hit = routes[:, :, None] == jnp.arange(experts, dtype=jnp.int32)
    return jnp.sum(jnp.where(hit, gates[:, :, None], 0), axis=1).astype(jnp.bfloat16)


def summed(*terms):
    total = terms[0].astype(jnp.float32)
    for term in terms[1:]:
        total = total + term.astype(jnp.float32)
    return total.astype(jnp.bfloat16)


def rows_of(*pieces):
    return jnp.concatenate(pieces, axis=0)


def first_sends(part):
    half = part.shape[-1] // 2
    return part[..., :half], part[..., half:]


def dense_plan(tokens, out_grad, routes, gates, w_gate, w_up, w_down):
    rows, features = tokens.shape
    experts = lax.axis_size("expert")
    half = features // 2
    gate_w, up_w, down_w = w_gate[0], w_up[0], w_down[0]
    own = jnp.arange(LANES, dtype=jnp.int32) == lax.axis_index("expert")

    def expert_rows(near, far, near_other, far_other):
        x_rows = rows_of(near[0], far[0], near_other[0], far_other[0])[:, :features]
        g_rows = rows_of(near[1], far[1], near_other[1], far_other[1])
        scale = g_rows[:, features:].astype(jnp.float32)
        scale = jnp.sum(jnp.where(own, scale, 0.0), axis=-1, keepdims=True)
        g_rows = g_rows[:, :features]
        gate_pre = jnp.einsum("rd,fd->rf", x_rows, gate_w, preferred_element_type=jnp.float32)
        up_pre = jnp.einsum("rd,fd->rf", x_rows, up_w, preferred_element_type=jnp.float32)
        d_hidden = scale * jnp.einsum("rd,fd->rf", g_rows, down_w, preferred_element_type=jnp.float32)
        sigmoid_gate = jax.nn.sigmoid(gate_pre)
        silu_gate = gate_pre * sigmoid_gate
        hidden = (scale * silu_gate * up_pre).astype(jnp.bfloat16)
        d_up_act = (d_hidden * silu_gate).astype(jnp.bfloat16)
        d_gate_act = (
            d_hidden * up_pre * sigmoid_gate * (1.0 + gate_pre * (1.0 - sigmoid_gate))
        ).astype(jnp.bfloat16)
        part = jnp.einsum("rf,fd->rd", d_gate_act, gate_w, preferred_element_type=jnp.float32)
        part = part + jnp.einsum("rf,fd->rd", d_up_act, up_w, preferred_element_type=jnp.float32)
        part = part.astype(jnp.bfloat16).reshape(2, 8, rows, features)
        return part, (x_rows, g_rows, hidden, d_gate_act, d_up_act)

    def near_of(mine, from_x, from_y, from_z):
        return jnp.concatenate([mine, from_x, from_y, from_z], axis=1)

    def far_of(second_x, second_y, second_z, third_x, third_y):
        return jnp.stack(
            [
                rows_of(second_y[0], second_y[1], second_z[0], third_y),
                rows_of(second_x[0], second_z[1], second_x[1], third_x),
            ]
        )

    def firsts(mine):
        return over_x(mine), over_y(mine), over_z(mine)

    def seconds(from_x, from_y, from_z):
        return (
            over_x(jnp.stack([from_y[1], from_z[1]])),
            over_y(jnp.stack([from_x[0], from_z[0]])),
            over_z(jnp.stack([from_x[0], from_y[1]])),
        )

    def thirds(second_z):
        return over_x(second_z[1]), over_y(second_z[0])

    scales = gate_of_expert(routes, gates, experts)
    scales = jnp.pad(scales, ((0, 0), (0, LANES - experts)))
    mine = jnp.stack([jnp.pad(tokens, ((0, 0), (0, LANES))), jnp.concatenate([out_grad, scales], axis=1)])
    first = firsts(mine)
    distant = over_far_z(mine)
    first = together(first)
    second = seconds(*first)
    near = near_of(mine, *first)
    near_other = over_core(near)
    second, near_other, distant = together((second, near_other, distant))
    first2 = firsts(distant)
    third = thirds(second[2])
    first2, third = together((first2, third))
    second2 = seconds(*first2)
    far = far_of(*second, *third)
    far_other = over_core(far)
    near2 = near_of(distant, *first2)
    near2_other = over_core(near2)
    part, kept = expert_rows(near, far, near_other, far_other)
    second2, near2_other, part = together((second2, near2_other, part))
    third2 = thirds(second2[2])
    part_other = over_core(part[1])
    third2, part_other = together((third2, part_other))
    far2 = far_of(*second2, *third2)
    far2_other = over_core(far2)

    def lane_sums(part, part_other):
        own, x, y, z, xy, yz, xz, xyz = (summed(part[i], part_other[i]) for i in range(8))
        opening = over_x(xyz[:, half:]), over_y(xyz[:, :half])
        middle = over_x(jnp.stack([xy[:, half:], xz[:, half:]])), over_y(jnp.stack([xy[:, :half], yz[:, :half]]))
        return (own, x, y, z, yz[:, half:], xz[:, :half]), opening, middle

    def sent_z(sums, opening):
        return over_z(jnp.concatenate([summed(sums[5], opening[1]), summed(sums[4], opening[0])], axis=1))

    def last_sends(sums, middle, from_z):
        _, x, y, z, _, _ = sums
        from_x, from_y = middle
        x = jnp.concatenate([summed(x[:, :half], from_y[0], from_z[:, :half]), x[:, half:]], axis=1)
        y = jnp.concatenate([y[:, :half], summed(y[:, half:], from_x[0], from_z[:, half:])], axis=1)
        z = jnp.concatenate([summed(z[:, :half], from_y[1]), summed(z[:, half:], from_x[1])], axis=1)
        return over_x(x), over_y(y), over_z(z)

    sums, opening, middle = lane_sums(part[0], part_other)
    opening, far2_other = together((opening, far2_other))
    from_z = sent_z(sums, opening)
    part2, kept2 = expert_rows(near2, far2, near2_other, far2_other)
    middle, from_z, part2 = together((middle, from_z, part2))
    part2_other = over_core(part2[1])
    last = last_sends(sums, middle, from_z)
    last, part2_other = together((last, part2_other))
    near_total = summed(sums[0], *last)
    sums2, opening2, middle2 = lane_sums(part2[0], part2_other)
    from_z2 = sent_z(sums2, opening2)
    last2 = last_sends(sums2, middle2, from_z2)
    d_tokens = summed(near_total, over_far_z(summed(sums2[0], *last2)))

    def weight_grad(at, side):
        return jnp.einsum(
            "rf,rd->fd",
            rows_of(kept[at], kept2[at]),
            rows_of(kept[side], kept2[side]),
            preferred_element_type=jnp.float32,
        ).astype(jnp.bfloat16)[None]

    return d_tokens, weight_grad(3, 0), weight_grad(4, 0), weight_grad(2, 1)


def per_device(tokens, out_grad, routes, gates, w_gate, w_up, w_down):
    tok_rows, top_count = routes.shape
    experts = lax.axis_size("expert")
    capacity = max(2, min(tok_rows, 3 * tok_rows * top_count // (2 * experts)))
    crowded = 2 * capacity >= tok_rows and lax.axis_size("dp") == 2 and experts == 16
    plan = dense_plan if crowded else slot_plan
    return plan(tokens, out_grad, routes, gates, w_gate, w_up, w_down)


def solution(mesh):
    in_specs = (
        P(("dp", "expert"), None),
        P(("dp", "expert"), None),
        P(("dp", "expert"), None),
        P(("dp", "expert"), None),
        P("expert", "dp", None),
        P("expert", "dp", None),
        P("expert", "dp", None),
    )
    out_specs = (
        P(("dp", "expert"), None),
        P("expert", "dp", None),
        P("expert", "dp", None),
        P("expert", "dp", None),
    )
    return jax.shard_map(
        per_device, mesh=mesh, in_specs=in_specs, out_specs=out_specs, check_vma=False
    )
```

```python
from functools import partial

import jax
import jax.numpy as jnp
from jax import lax
from jax.sharding import PartitionSpec as P


def cell_match(routes, experts, capacity):
    expert_ids = jnp.arange(experts, dtype=jnp.int32)
    onehot = (routes[:, :, None] == expert_ids).astype(jnp.int32)
    chosen = jnp.sum(onehot, axis=1)
    earlier = jnp.cumsum(chosen, axis=0) - chosen
    slot_index = jnp.sum(onehot * earlier[:, None, :], axis=2)
    target = routes * capacity + slot_index
    cell_ids = jnp.arange(experts * capacity, dtype=jnp.int32)
    return target[:, :, None] == cell_ids


def placement(matches, experts, capacity):
    return jnp.any(matches, axis=1).reshape(-1, experts, capacity).astype(jnp.bfloat16)


def weighting(matches, gates, experts, capacity):
    spread = jnp.where(matches, gates.astype(jnp.float32)[:, :, None], 0.0)
    return jnp.sum(spread, axis=1).reshape(-1, experts, capacity)


def slot_plan(tokens, out_grad, routes, gates, w_gate, w_up, w_down):
    tok_rows, features = tokens.shape
    top_count = routes.shape[1]
    experts = lax.axis_size("expert")
    groups = lax.axis_size("dp")
    capacity = max(2, min(tok_rows, 3 * tok_rows * top_count // (2 * experts)))
    match_fn = partial(cell_match, experts=experts, capacity=capacity)
    place_fn = partial(placement, experts=experts, capacity=capacity)
    weight_fn = partial(weighting, experts=experts, capacity=capacity)
    own_match = match_fn(routes)
    own_place = place_fn(own_match)
    own_weight = weight_fn(own_match, gates)
    input_send = jnp.einsum(
        "tec,td->ecd", own_place, tokens, preferred_element_type=jnp.float32
    ).astype(jnp.bfloat16)
    grad_send = jnp.einsum(
        "tec,td->ecd", own_weight, out_grad.astype(jnp.float32), precision=lax.Precision.HIGHEST
    ).astype(jnp.bfloat16)
    input_recv, grad_recv = (
        lax.all_to_all(input_send, "expert", split_axis=0, concat_axis=0, tiled=True),
        lax.all_to_all(grad_send, "expert", split_axis=0, concat_axis=0, tiled=True),
    )
    input_recv = input_recv.reshape(experts, 1, capacity, features)
    grad_recv = grad_recv.reshape(experts, 1, capacity, features)
    input_slots, grad_slots = (
        lax.all_gather(input_recv, "dp", axis=1, tiled=True),
        lax.all_gather(grad_recv, "dp", axis=1, tiled=True),
    )
    input_rows = input_slots.reshape(-1, features)
    grad_rows = grad_slots.reshape(-1, features)
    gate_w = w_gate[0]
    up_w = w_up[0]
    down_w = w_down[0]
    gate_pre = jnp.einsum("rd,fd->rf", input_rows, gate_w, preferred_element_type=jnp.float32)
    up_pre = jnp.einsum("rd,fd->rf", input_rows, up_w, preferred_element_type=jnp.float32)
    sigmoid_gate = jax.nn.sigmoid(gate_pre)
    silu_gate = gate_pre * sigmoid_gate
    hidden = (silu_gate * up_pre).astype(jnp.bfloat16)
    d_hidden = jnp.einsum("rd,fd->rf", grad_rows, down_w, preferred_element_type=jnp.float32)
    d_up_act = (d_hidden * silu_gate).astype(jnp.bfloat16)
    d_gate_act = (
        d_hidden * up_pre * sigmoid_gate * (1.0 + gate_pre * (1.0 - sigmoid_gate))
    ).astype(jnp.bfloat16)
    grad_down = jnp.einsum(
        "rf,rd->fd", hidden, grad_rows, preferred_element_type=jnp.float32
    ).astype(jnp.bfloat16)
    grad_gate = jnp.einsum(
        "rf,rd->fd", d_gate_act, input_rows, preferred_element_type=jnp.float32
    ).astype(jnp.bfloat16)
    grad_up = jnp.einsum(
        "rf,rd->fd", d_up_act, input_rows, preferred_element_type=jnp.float32
    ).astype(jnp.bfloat16)
    partial_sum = jnp.einsum("rf,fd->rd", d_gate_act, gate_w, preferred_element_type=jnp.float32)
    partial_sum = partial_sum + jnp.einsum(
        "rf,fd->rd", d_up_act, up_w, preferred_element_type=jnp.float32
    )
    rounded = partial_sum.astype(jnp.bfloat16).reshape(experts, groups, capacity, features)
    held = lax.optimization_barrier(rounded).astype(jnp.float32)
    slot_total = lax.psum_scatter(
        held.astype(jnp.bfloat16), "dp", scatter_dimension=1, tiled=True
    ).astype(jnp.float32)
    returned = lax.all_to_all(
        slot_total[:, 0].astype(jnp.bfloat16), "expert", split_axis=0, concat_axis=0, tiled=True
    ).astype(jnp.float32)
    summed = jnp.einsum(
        "tec,ecd->td", own_place.astype(jnp.float32), returned, precision=lax.Precision.HIGHEST
    )
    return (summed.astype(jnp.bfloat16), grad_gate[None], grad_up[None], grad_down[None])


def swapped(x, axis, bits):
    count = lax.axis_size(axis)
    return lax.ppermute(x, axis, [(i, i ^ bits) for i in range(count)])


over_core = partial(swapped, axis="expert", bits=1)
over_x = partial(swapped, axis="expert", bits=2)
over_z = partial(swapped, axis="expert", bits=4)
over_far_z = partial(swapped, axis="expert", bits=8)
over_y = partial(swapped, axis="dp", bits=1)
together = lax.optimization_barrier
LANES = 128


def gate_of_expert(routes, gates, experts):
    hit = routes[:, :, None] == jnp.arange(experts, dtype=jnp.int32)
    return jnp.sum(jnp.where(hit, gates[:, :, None], 0), axis=1).astype(jnp.bfloat16)


def summed(*terms):
    total = terms[0].astype(jnp.float32)
    for term in terms[1:]:
        total = total + term.astype(jnp.float32)
    return total.astype(jnp.bfloat16)


def rows_of(*pieces):
    return jnp.concatenate(pieces, axis=0)


def first_sends(part):
    half = part.shape[-1] // 2
    return part[..., :half], part[..., half:]


def dense_plan(tokens, out_grad, routes, gates, w_gate, w_up, w_down):
    rows, features = tokens.shape
    experts = lax.axis_size("expert")
    half = features // 2
    gate_w, up_w, down_w = w_gate[0], w_up[0], w_down[0]
    own = jnp.arange(LANES, dtype=jnp.int32) == lax.axis_index("expert")

    def expert_rows(lane, other):
        x_rows = rows_of(lane[0], other[0])[:, :features]
        g_rows = rows_of(lane[1], other[1])
        scale = g_rows[:, features:].astype(jnp.float32)
        scale = jnp.sum(jnp.where(own, scale, 0.0), axis=-1, keepdims=True)
        g_rows = g_rows[:, :features]
        gate_pre = jnp.einsum("rd,fd->rf", x_rows, gate_w, preferred_element_type=jnp.float32)
        up_pre = jnp.einsum("rd,fd->rf", x_rows, up_w, preferred_element_type=jnp.float32)
        d_hidden = scale * jnp.einsum("rd,fd->rf", g_rows, down_w, preferred_element_type=jnp.float32)
        sigmoid_gate = jax.nn.sigmoid(gate_pre)
        silu_gate = gate_pre * sigmoid_gate
        hidden = (scale * silu_gate * up_pre).astype(jnp.bfloat16)
        d_up_act = (d_hidden * silu_gate).astype(jnp.bfloat16)
        d_gate_act = (
            d_hidden * up_pre * sigmoid_gate * (1.0 + gate_pre * (1.0 - sigmoid_gate))
        ).astype(jnp.bfloat16)
        part = jnp.einsum("rf,fd->rd", d_gate_act, gate_w, preferred_element_type=jnp.float32)
        part = part + jnp.einsum("rf,fd->rd", d_up_act, up_w, preferred_element_type=jnp.float32)
        part = part.astype(jnp.bfloat16).reshape(2, 4, rows, features)
        return part, (x_rows, g_rows, hidden, d_gate_act, d_up_act)

    def near_of(mine, from_x, from_y, from_z):
        return jnp.concatenate([mine, from_x, from_y, from_z], axis=1)

    def far_of(second_x, second_y, second_z, third_x, third_y):
        return jnp.stack(
            [
                rows_of(second_y[0], second_y[1], second_z[0], third_y),
                rows_of(second_x[0], second_z[1], second_x[1], third_x),
            ]
        )

    def firsts(mine):
        return over_x(mine), over_y(mine), over_z(mine)

    def seconds(from_x, from_y, from_z):
        return (
            over_x(jnp.stack([from_y[1], from_z[1]])),
            over_y(jnp.stack([from_x[0], from_z[0]])),
            over_z(jnp.stack([from_x[0], from_y[1]])),
        )

    def thirds(second_z):
        return over_x(second_z[1]), over_y(second_z[0])

    scales = gate_of_expert(routes, gates, experts)
    scales = jnp.pad(scales, ((0, 0), (0, LANES - experts)))
    mine = jnp.stack([jnp.pad(tokens, ((0, 0), (0, LANES))), jnp.concatenate([out_grad, scales], axis=1)])
    from_x, from_y, from_z = firsts(mine)
    distant = over_far_z(mine)
    from_x, from_y = together((from_x, from_y))
    g_far, t_far = over_x(from_y[1]), over_y(from_x[0])
    from_z, g_far, t_far = together((from_z, g_far, t_far))
    z_x, z_y = over_x(from_z), over_y(from_z)
    near = near_of(mine, from_x, from_y, from_z)
    near_other = over_core(near)
    z_x, z_y, near_other, distant = together((z_x, z_y, near_other, distant))
    first2 = firsts(distant)
    third = over_x(z_y[1]), over_y(z_x[0])
    part_near, kept_near = expert_rows(near, near_other)
    first2, third, part_near = together((first2, third, part_near))
    second2 = seconds(*first2)
    far = jnp.stack(
        [rows_of(t_far, z_y[0], z_x[0], third[1]), rows_of(g_far, z_y[1], z_x[1], third[0])]
    )
    far_other = over_core(far)
    near2 = near_of(distant, *first2)
    near2_other = over_core(near2)
    part_far, kept_far = expert_rows(far, far_other)
    second2, near2_other, part_far = together((second2, near2_other, part_far))
    third2 = thirds(second2[2])
    others = over_core(part_near[1]), over_core(part_far[1])
    part_near2, kept_near2 = expert_rows(near2, near2_other)
    third2, others, part_near2 = together((third2, others, part_near2))
    far2 = far_of(*second2, *third2)
    far2_other = over_core(far2)

    def lane_sums(near_part, far_part, near_part_other, far_part_other):
        return tuple(summed(near_part[i], near_part_other[i]) for i in range(4)) + tuple(
            summed(far_part[i], far_part_other[i]) for i in range(4)
        )

    def opening_sends(sums):
        return over_x(sums[7][:, half:]), over_y(sums[7][:, :half])

    def middle_sends(sums):
        _, _, _, _, xy, yz, xz, _ = sums
        return over_x(jnp.stack([xy[:, half:], xz[:, half:]])), over_y(jnp.stack([xy[:, :half], yz[:, :half]]))

    def early_sends(sums):
        _, _, _, _, xy, yz, xz, xyz = sums
        in_x = over_x(jnp.stack([xyz[:, half:], xy[:, half:], xz[:, half:]]))
        in_y = over_y(jnp.stack([xyz[:, :half], xy[:, :half], yz[:, :half]]))
        return in_x, in_y

    def sent_z(sums, opening):
        _, _, _, _, _, yz, xz, _ = sums
        return over_z(jnp.concatenate([summed(xz[:, :half], opening[1]), summed(yz[:, half:], opening[0])], axis=1))

    def last_sends(sums, middle, from_z):
        _, x, y, z, _, _, _, _ = sums
        from_x, from_y = middle
        x = jnp.concatenate([summed(x[:, :half], from_y[0], from_z[:, :half]), x[:, half:]], axis=1)
        y = jnp.concatenate([y[:, :half], summed(y[:, half:], from_x[0], from_z[:, half:])], axis=1)
        z = jnp.concatenate([summed(z[:, :half], from_y[1]), summed(z[:, half:], from_x[1])], axis=1)
        return over_x(x), over_y(y), over_z(z)

    sums = lane_sums(part_near[0], part_far[0], *others)
    in_x, in_y = early_sends(sums)
    part_far2, kept_far2 = expert_rows(far2, far2_other)
    part_far2, in_x, in_y = together((part_far2, in_x, in_y))
    others2 = over_core(part_near2[1]), over_core(part_far2[1])
    middle = in_x[1:], in_y[1:]
    from_z = sent_z(sums, (in_x[0], in_y[0]))
    sums2 = lane_sums(part_near2[0], part_far2[0], *others2)
    opening2, middle2 = opening_sends(sums2), middle_sends(sums2)
    from_z2 = sent_z(sums2, opening2)
    last2 = last_sends(sums2, middle2, from_z2)
    sums, middle, from_z, last2 = together((sums, middle, from_z, last2))
    returned = over_far_z(summed(sums2[0], *last2))
    last = last_sends(sums, middle, from_z)
    d_tokens = summed(sums[0], *last, returned)

    def weight_grad(at, side):
        kept = (kept_near, kept_far, kept_near2, kept_far2)
        return jnp.einsum(
            "rf,rd->fd",
            rows_of(*(held[at] for held in kept)),
            rows_of(*(held[side] for held in kept)),
            preferred_element_type=jnp.float32,
        ).astype(jnp.bfloat16)[None]

    return d_tokens, weight_grad(3, 0), weight_grad(4, 0), weight_grad(2, 1)


def per_device(tokens, out_grad, routes, gates, w_gate, w_up, w_down):
    tok_rows, top_count = routes.shape
    experts = lax.axis_size("expert")
    capacity = max(2, min(tok_rows, 3 * tok_rows * top_count // (2 * experts)))
    crowded = 2 * capacity >= tok_rows and lax.axis_size("dp") == 2 and experts == 16
    plan = dense_plan if crowded else slot_plan
    return plan(tokens, out_grad, routes, gates, w_gate, w_up, w_down)


def solution(mesh):
    in_specs = (
        P(("dp", "expert"), None),
        P(("dp", "expert"), None),
        P(("dp", "expert"), None),
        P(("dp", "expert"), None),
        P("expert", "dp", None),
        P("expert", "dp", None),
        P("expert", "dp", None),
    )
    out_specs = (
        P(("dp", "expert"), None),
        P("expert", "dp", None),
        P("expert", "dp", None),
        P("expert", "dp", None),
    )
    return jax.shard_map(
        per_device, mesh=mesh, in_specs=in_specs, out_specs=out_specs, check_vma=False
    )
```

```python
from functools import partial

import jax
import jax.numpy as jnp
from jax import lax
from jax.sharding import PartitionSpec as P


def cell_match(routes, experts, capacity):
    expert_ids = jnp.arange(experts, dtype=jnp.int32)
    onehot = (routes[:, :, None] == expert_ids).astype(jnp.int32)
    chosen = jnp.sum(onehot, axis=1)
    earlier = jnp.cumsum(chosen, axis=0) - chosen
    slot_index = jnp.sum(onehot * earlier[:, None, :], axis=2)
    target = routes * capacity + slot_index
    cell_ids = jnp.arange(experts * capacity, dtype=jnp.int32)
    return target[:, :, None] == cell_ids


def placement(matches, experts, capacity):
    return jnp.any(matches, axis=1).reshape(-1, experts, capacity).astype(jnp.bfloat16)


def weighting(matches, gates, experts, capacity):
    spread = jnp.where(matches, gates.astype(jnp.float32)[:, :, None], 0.0)
    return jnp.sum(spread, axis=1).reshape(-1, experts, capacity)


def slot_plan(tokens, out_grad, routes, gates, w_gate, w_up, w_down):
    tok_rows, features = tokens.shape
    top_count = routes.shape[1]
    experts = lax.axis_size("expert")
    groups = lax.axis_size("dp")
    capacity = max(2, min(tok_rows, 3 * tok_rows * top_count // (2 * experts)))
    match_fn = partial(cell_match, experts=experts, capacity=capacity)
    place_fn = partial(placement, experts=experts, capacity=capacity)
    weight_fn = partial(weighting, experts=experts, capacity=capacity)
    own_match = match_fn(routes)
    own_place = place_fn(own_match)
    own_weight = weight_fn(own_match, gates)
    input_send = jnp.einsum(
        "tec,td->ecd", own_place, tokens, preferred_element_type=jnp.float32
    ).astype(jnp.bfloat16)
    grad_send = jnp.einsum(
        "tec,td->ecd", own_weight, out_grad.astype(jnp.float32), precision=lax.Precision.HIGHEST
    ).astype(jnp.bfloat16)
    input_recv, grad_recv = (
        lax.all_to_all(input_send, "expert", split_axis=0, concat_axis=0, tiled=True),
        lax.all_to_all(grad_send, "expert", split_axis=0, concat_axis=0, tiled=True),
    )
    input_recv = input_recv.reshape(experts, 1, capacity, features)
    grad_recv = grad_recv.reshape(experts, 1, capacity, features)
    input_slots, grad_slots = (
        lax.all_gather(input_recv, "dp", axis=1, tiled=True),
        lax.all_gather(grad_recv, "dp", axis=1, tiled=True),
    )
    input_rows = input_slots.reshape(-1, features)
    grad_rows = grad_slots.reshape(-1, features)
    gate_w = w_gate[0]
    up_w = w_up[0]
    down_w = w_down[0]
    gate_pre = jnp.einsum("rd,fd->rf", input_rows, gate_w, preferred_element_type=jnp.float32)
    up_pre = jnp.einsum("rd,fd->rf", input_rows, up_w, preferred_element_type=jnp.float32)
    sigmoid_gate = jax.nn.sigmoid(gate_pre)
    silu_gate = gate_pre * sigmoid_gate
    hidden = (silu_gate * up_pre).astype(jnp.bfloat16)
    d_hidden = jnp.einsum("rd,fd->rf", grad_rows, down_w, preferred_element_type=jnp.float32)
    d_up_act = (d_hidden * silu_gate).astype(jnp.bfloat16)
    d_gate_act = (
        d_hidden * up_pre * sigmoid_gate * (1.0 + gate_pre * (1.0 - sigmoid_gate))
    ).astype(jnp.bfloat16)
    grad_down = jnp.einsum(
        "rf,rd->fd", hidden, grad_rows, preferred_element_type=jnp.float32
    ).astype(jnp.bfloat16)
    grad_gate = jnp.einsum(
        "rf,rd->fd", d_gate_act, input_rows, preferred_element_type=jnp.float32
    ).astype(jnp.bfloat16)
    grad_up = jnp.einsum(
        "rf,rd->fd", d_up_act, input_rows, preferred_element_type=jnp.float32
    ).astype(jnp.bfloat16)
    partial_sum = jnp.einsum("rf,fd->rd", d_gate_act, gate_w, preferred_element_type=jnp.float32)
    partial_sum = partial_sum + jnp.einsum(
        "rf,fd->rd", d_up_act, up_w, preferred_element_type=jnp.float32
    )
    rounded = partial_sum.astype(jnp.bfloat16).reshape(experts, groups, capacity, features)
    held = lax.optimization_barrier(rounded).astype(jnp.float32)
    slot_total = lax.psum_scatter(
        held.astype(jnp.bfloat16), "dp", scatter_dimension=1, tiled=True
    ).astype(jnp.float32)
    returned = lax.all_to_all(
        slot_total[:, 0].astype(jnp.bfloat16), "expert", split_axis=0, concat_axis=0, tiled=True
    ).astype(jnp.float32)
    summed = jnp.einsum(
        "tec,ecd->td", own_place.astype(jnp.float32), returned, precision=lax.Precision.HIGHEST
    )
    return (summed.astype(jnp.bfloat16), grad_gate[None], grad_up[None], grad_down[None])


def swapped(x, axis, bits):
    count = lax.axis_size(axis)
    return lax.ppermute(x, axis, [(i, i ^ bits) for i in range(count)])


over_core = partial(swapped, axis="expert", bits=1)
over_x = partial(swapped, axis="expert", bits=2)
over_z = partial(swapped, axis="expert", bits=4)
over_far_z = partial(swapped, axis="expert", bits=8)
over_y = partial(swapped, axis="dp", bits=1)
together = lax.optimization_barrier
LANES = 128


def gate_of_expert(routes, gates, experts):
    hit = routes[:, :, None] == jnp.arange(experts, dtype=jnp.int32)
    return jnp.sum(jnp.where(hit, gates[:, :, None], 0), axis=1).astype(jnp.bfloat16)


def summed(*terms):
    total = terms[0].astype(jnp.float32)
    for term in terms[1:]:
        total = total + term.astype(jnp.float32)
    return total.astype(jnp.bfloat16)


def rows_of(*pieces):
    return jnp.concatenate(pieces, axis=0)


def first_sends(part):
    half = part.shape[-1] // 2
    return part[..., :half], part[..., half:]


def dense_plan(tokens, out_grad, routes, gates, w_gate, w_up, w_down):
    rows, features = tokens.shape
    experts = lax.axis_size("expert")
    half = features // 2
    gate_w, up_w, down_w = w_gate[0], w_up[0], w_down[0]
    own = jnp.arange(LANES, dtype=jnp.int32) == lax.axis_index("expert")

    def expert_rows(lane, other):
        x_rows = rows_of(lane[0], other[0])[:, :features]
        g_rows = rows_of(lane[1], other[1])
        scale = g_rows[:, features:].astype(jnp.float32)
        scale = jnp.sum(jnp.where(own, scale, 0.0), axis=-1, keepdims=True)
        g_rows = g_rows[:, :features]
        gate_pre = jnp.einsum("rd,fd->rf", x_rows, gate_w, preferred_element_type=jnp.float32)
        up_pre = jnp.einsum("rd,fd->rf", x_rows, up_w, preferred_element_type=jnp.float32)
        d_hidden = scale * jnp.einsum("rd,fd->rf", g_rows, down_w, preferred_element_type=jnp.float32)
        sigmoid_gate = jax.nn.sigmoid(gate_pre)
        silu_gate = gate_pre * sigmoid_gate
        hidden = (scale * silu_gate * up_pre).astype(jnp.bfloat16)
        d_up_act = (d_hidden * silu_gate).astype(jnp.bfloat16)
        d_gate_act = (
            d_hidden * up_pre * sigmoid_gate * (1.0 + gate_pre * (1.0 - sigmoid_gate))
        ).astype(jnp.bfloat16)
        part = jnp.einsum("rf,fd->rd", d_gate_act, gate_w, preferred_element_type=jnp.float32)
        part = part + jnp.einsum("rf,fd->rd", d_up_act, up_w, preferred_element_type=jnp.float32)
        part = part.astype(jnp.bfloat16).reshape(2, 4, rows, features)
        return part, (x_rows, g_rows, hidden, d_gate_act, d_up_act)

    def near_of(mine, from_x, from_y, from_z):
        return jnp.concatenate([mine, from_x, from_y, from_z], axis=1)

    def far_of(second_x, second_y, second_z, third_x, third_y):
        return jnp.stack(
            [
                rows_of(second_y[0], second_y[1], second_z[0], third_y),
                rows_of(second_x[0], second_z[1], second_x[1], third_x),
            ]
        )

    def firsts(mine):
        return over_x(mine), over_y(mine), over_z(mine)

    def seconds(from_x, from_y, from_z):
        return (
            over_x(jnp.stack([from_y[1], from_z[1]])),
            over_y(jnp.stack([from_x[0], from_z[0]])),
            over_z(jnp.stack([from_x[0], from_y[1]])),
        )

    def thirds(second_z):
        return over_x(second_z[1]), over_y(second_z[0])

    scales = gate_of_expert(routes, gates, experts)
    scales = jnp.pad(scales, ((0, 0), (0, LANES - experts)))
    tail = ((0, 0), (0, LANES))
    grad_rows = jnp.concatenate([out_grad, scales], axis=1)
    mine = jnp.stack([jnp.pad(tokens, tail), grad_rows])
    from_x, from_y, from_z = firsts(mine)
    distant_t = over_far_z(tokens)
    mine, distant_t = together((mine, distant_t))
    distant_g = over_far_z(mine[1])
    from_x, from_y = together((from_x, from_y))
    g_far, t_far = over_x(from_y[1]), over_y(from_x[0])
    from_z, g_far, t_far = together((from_z, g_far, t_far))
    z_x, z_y = over_x(from_z), over_y(from_z)
    near = near_of(mine, from_x, from_y, from_z)
    near_other = over_core(near)
    z_x, z_y, near_other, distant_t, distant_g = together((z_x, z_y, near_other, distant_t, distant_g))
    distant = jnp.stack([jnp.pad(distant_t, tail), distant_g])
    first2 = firsts(distant)
    third = over_x(z_y[1]), over_y(z_x[0])
    part_near, kept_near = expert_rows(near, near_other)
    first2, third, part_near = together((first2, third, part_near))
    second2 = seconds(*first2)
    far = jnp.stack(
        [rows_of(t_far, z_y[0], z_x[0], third[1]), rows_of(g_far, z_y[1], z_x[1], third[0])]
    )
    far_other = over_core(far)
    near2 = near_of(distant, *first2)
    near2_other = over_core(near2)
    part_far, kept_far = expert_rows(far, far_other)
    second2, near2_other, part_far = together((second2, near2_other, part_far))
    third2 = thirds(second2[2])
    others = over_core(part_near[1]), over_core(part_far[1])
    part_near2, kept_near2 = expert_rows(near2, near2_other)
    third2, others, part_near2 = together((third2, others, part_near2))
    far2 = far_of(*second2, *third2)
    far2_other = over_core(far2)

    def lane_sums(near_part, far_part, near_part_other, far_part_other):
        return tuple(summed(near_part[i], near_part_other[i]) for i in range(4)) + tuple(
            summed(far_part[i], far_part_other[i]) for i in range(4)
        )

    def opening_sends(sums):
        return over_x(sums[7][:, half:]), over_y(sums[7][:, :half])

    def middle_sends(sums):
        _, _, _, _, xy, yz, xz, _ = sums
        return over_x(jnp.stack([xy[:, half:], xz[:, half:]])), over_y(jnp.stack([xy[:, :half], yz[:, :half]]))

    def early_sends(sums):
        _, _, _, _, xy, yz, xz, xyz = sums
        in_x = over_x(jnp.stack([xyz[:, half:], xy[:, half:], xz[:, half:]]))
        in_y = over_y(jnp.stack([xyz[:, :half], xy[:, :half], yz[:, :half]]))
        return in_x, in_y

    def sent_z(sums, opening):
        _, _, _, _, _, yz, xz, _ = sums
        return over_z(jnp.concatenate([summed(xz[:, :half], opening[1]), summed(yz[:, half:], opening[0])], axis=1))

    def last_sends(sums, middle, from_z):
        _, x, y, z, _, _, _, _ = sums
        from_x, from_y = middle
        x = jnp.concatenate([summed(x[:, :half], from_y[0], from_z[:, :half]), x[:, half:]], axis=1)
        y = jnp.concatenate([y[:, :half], summed(y[:, half:], from_x[0], from_z[:, half:])], axis=1)
        z = jnp.concatenate([summed(z[:, :half], from_y[1]), summed(z[:, half:], from_x[1])], axis=1)
        return over_x(x), over_y(y), over_z(z)

    sums = lane_sums(part_near[0], part_far[0], *others)
    in_x, in_y = early_sends(sums)
    part_far2, kept_far2 = expert_rows(far2, far2_other)
    part_far2, in_x, in_y = together((part_far2, in_x, in_y))
    others2 = over_core(part_near2[1]), over_core(part_far2[1])
    middle = in_x[1:], in_y[1:]
    from_z = sent_z(sums, (in_x[0], in_y[0]))
    sums2 = lane_sums(part_near2[0], part_far2[0], *others2)
    opening2, middle2 = opening_sends(sums2), middle_sends(sums2)
    from_z2 = sent_z(sums2, opening2)
    last2 = last_sends(sums2, middle2, from_z2)
    sums, middle, from_z, last2 = together((sums, middle, from_z, last2))
    returned = over_far_z(summed(sums2[0], *last2))
    last = last_sends(sums, middle, from_z)
    d_tokens = summed(sums[0], *last, returned)

    def weight_grad(at, side):
        kept = (kept_near, kept_far, kept_near2, kept_far2)
        return jnp.einsum(
            "rf,rd->fd",
            rows_of(*(held[at] for held in kept)),
            rows_of(*(held[side] for held in kept)),
            preferred_element_type=jnp.float32,
        ).astype(jnp.bfloat16)[None]

    return d_tokens, weight_grad(3, 0), weight_grad(4, 0), weight_grad(2, 1)


def per_device(tokens, out_grad, routes, gates, w_gate, w_up, w_down):
    tok_rows, top_count = routes.shape
    experts = lax.axis_size("expert")
    capacity = max(2, min(tok_rows, 3 * tok_rows * top_count // (2 * experts)))
    crowded = 2 * capacity >= tok_rows and lax.axis_size("dp") == 2 and experts == 16
    plan = dense_plan if crowded else slot_plan
    return plan(tokens, out_grad, routes, gates, w_gate, w_up, w_down)


def solution(mesh):
    in_specs = (
        P(("dp", "expert"), None),
        P(("dp", "expert"), None),
        P(("dp", "expert"), None),
        P(("dp", "expert"), None),
        P("expert", "dp", None),
        P("expert", "dp", None),
        P("expert", "dp", None),
    )
    out_specs = (
        P(("dp", "expert"), None),
        P("expert", "dp", None),
        P("expert", "dp", None),
        P("expert", "dp", None),
    )
    return jax.shard_map(
        per_device, mesh=mesh, in_specs=in_specs, out_specs=out_specs, check_vma=False
    )
```

```python
from functools import partial

import jax
import jax.numpy as jnp
from jax import lax
from jax.sharding import PartitionSpec as P


def cell_match(routes, experts, capacity):
    expert_ids = jnp.arange(experts, dtype=jnp.int32)
    onehot = (routes[:, :, None] == expert_ids).astype(jnp.int32)
    chosen = jnp.sum(onehot, axis=1)
    earlier = jnp.cumsum(chosen, axis=0) - chosen
    slot_index = jnp.sum(onehot * earlier[:, None, :], axis=2)
    target = routes * capacity + slot_index
    cell_ids = jnp.arange(experts * capacity, dtype=jnp.int32)
    return target[:, :, None] == cell_ids


def placement(matches, experts, capacity):
    return jnp.any(matches, axis=1).reshape(-1, experts, capacity).astype(jnp.bfloat16)


def weighting(matches, gates, experts, capacity):
    spread = jnp.where(matches, gates.astype(jnp.float32)[:, :, None], 0.0)
    return jnp.sum(spread, axis=1).reshape(-1, experts, capacity)


def slot_plan(tokens, out_grad, routes, gates, w_gate, w_up, w_down):
    tok_rows, features = tokens.shape
    top_count = routes.shape[1]
    experts = lax.axis_size("expert")
    groups = lax.axis_size("dp")
    capacity = max(2, min(tok_rows, 3 * tok_rows * top_count // (2 * experts)))
    match_fn = partial(cell_match, experts=experts, capacity=capacity)
    place_fn = partial(placement, experts=experts, capacity=capacity)
    weight_fn = partial(weighting, experts=experts, capacity=capacity)
    own_match = match_fn(routes)
    own_place = place_fn(own_match)
    own_weight = weight_fn(own_match, gates)
    input_send = jnp.einsum(
        "tec,td->ecd", own_place, tokens, preferred_element_type=jnp.float32
    ).astype(jnp.bfloat16)
    grad_send = jnp.einsum(
        "tec,td->ecd", own_weight, out_grad.astype(jnp.float32), precision=lax.Precision.HIGHEST
    ).astype(jnp.bfloat16)
    input_recv, grad_recv = (
        lax.all_to_all(input_send, "expert", split_axis=0, concat_axis=0, tiled=True),
        lax.all_to_all(grad_send, "expert", split_axis=0, concat_axis=0, tiled=True),
    )
    input_recv = input_recv.reshape(experts, 1, capacity, features)
    grad_recv = grad_recv.reshape(experts, 1, capacity, features)
    input_slots, grad_slots = (
        lax.all_gather(input_recv, "dp", axis=1, tiled=True),
        lax.all_gather(grad_recv, "dp", axis=1, tiled=True),
    )
    input_rows = input_slots.reshape(-1, features)
    grad_rows = grad_slots.reshape(-1, features)
    gate_w = w_gate[0]
    up_w = w_up[0]
    down_w = w_down[0]
    gate_pre = jnp.einsum("rd,fd->rf", input_rows, gate_w, preferred_element_type=jnp.float32)
    up_pre = jnp.einsum("rd,fd->rf", input_rows, up_w, preferred_element_type=jnp.float32)
    sigmoid_gate = jax.nn.sigmoid(gate_pre)
    silu_gate = gate_pre * sigmoid_gate
    hidden = (silu_gate * up_pre).astype(jnp.bfloat16)
    d_hidden = jnp.einsum("rd,fd->rf", grad_rows, down_w, preferred_element_type=jnp.float32)
    d_up_act = (d_hidden * silu_gate).astype(jnp.bfloat16)
    d_gate_act = (
        d_hidden * up_pre * sigmoid_gate * (1.0 + gate_pre * (1.0 - sigmoid_gate))
    ).astype(jnp.bfloat16)
    grad_down = jnp.einsum(
        "rf,rd->fd", hidden, grad_rows, preferred_element_type=jnp.float32
    ).astype(jnp.bfloat16)
    grad_gate = jnp.einsum(
        "rf,rd->fd", d_gate_act, input_rows, preferred_element_type=jnp.float32
    ).astype(jnp.bfloat16)
    grad_up = jnp.einsum(
        "rf,rd->fd", d_up_act, input_rows, preferred_element_type=jnp.float32
    ).astype(jnp.bfloat16)
    partial_sum = jnp.einsum("rf,fd->rd", d_gate_act, gate_w, preferred_element_type=jnp.float32)
    partial_sum = partial_sum + jnp.einsum(
        "rf,fd->rd", d_up_act, up_w, preferred_element_type=jnp.float32
    )
    rounded = partial_sum.astype(jnp.bfloat16).reshape(experts, groups, capacity, features)
    held = lax.optimization_barrier(rounded).astype(jnp.float32)
    slot_total = lax.psum_scatter(
        held.astype(jnp.bfloat16), "dp", scatter_dimension=1, tiled=True
    ).astype(jnp.float32)
    returned = lax.all_to_all(
        slot_total[:, 0].astype(jnp.bfloat16), "expert", split_axis=0, concat_axis=0, tiled=True
    ).astype(jnp.float32)
    summed = jnp.einsum(
        "tec,ecd->td", own_place.astype(jnp.float32), returned, precision=lax.Precision.HIGHEST
    )
    return (summed.astype(jnp.bfloat16), grad_gate[None], grad_up[None], grad_down[None])


def swapped(x, axis, bits):
    count = lax.axis_size(axis)
    return lax.ppermute(x, axis, [(i, i ^ bits) for i in range(count)])


over_core = partial(swapped, axis="expert", bits=1)
over_x = partial(swapped, axis="expert", bits=2)
over_z = partial(swapped, axis="expert", bits=4)
over_far_z = partial(swapped, axis="expert", bits=8)
over_y = partial(swapped, axis="dp", bits=1)
together = lax.optimization_barrier
LANES = 128


def gate_of_expert(routes, gates, experts):
    hit = routes[:, :, None] == jnp.arange(experts, dtype=jnp.int32)
    return jnp.sum(jnp.where(hit, gates[:, :, None], 0), axis=1).astype(jnp.bfloat16)


def summed(*terms):
    total = terms[0].astype(jnp.float32)
    for term in terms[1:]:
        total = total + term.astype(jnp.float32)
    return total.astype(jnp.bfloat16)


def rows_of(*pieces):
    return jnp.concatenate(pieces, axis=0)


def first_sends(part):
    half = part.shape[-1] // 2
    return part[..., :half], part[..., half:]


def dense_plan(tokens, out_grad, routes, gates, w_gate, w_up, w_down):
    rows, features = tokens.shape
    experts = lax.axis_size("expert")
    half = features // 2
    gate_w, up_w, down_w = w_gate[0], w_up[0], w_down[0]
    own = jnp.arange(LANES, dtype=jnp.int32) == lax.axis_index("expert")

    def expert_rows(lane, other):
        x_rows = rows_of(lane[0], other[0])[:, :features]
        g_rows = rows_of(lane[1], other[1])
        scale = g_rows[:, features:].astype(jnp.float32)
        scale = jnp.sum(jnp.where(own, scale, 0.0), axis=-1, keepdims=True)
        g_rows = g_rows[:, :features]
        gate_pre = jnp.einsum("rd,fd->rf", x_rows, gate_w, preferred_element_type=jnp.float32)
        up_pre = jnp.einsum("rd,fd->rf", x_rows, up_w, preferred_element_type=jnp.float32)
        d_hidden = scale * jnp.einsum("rd,fd->rf", g_rows, down_w, preferred_element_type=jnp.float32)
        sigmoid_gate = jax.nn.sigmoid(gate_pre)
        silu_gate = gate_pre * sigmoid_gate
        hidden = (scale * silu_gate * up_pre).astype(jnp.bfloat16)
        d_up_act = (d_hidden * silu_gate).astype(jnp.bfloat16)
        d_gate_act = (
            d_hidden * up_pre * sigmoid_gate * (1.0 + gate_pre * (1.0 - sigmoid_gate))
        ).astype(jnp.bfloat16)
        part = jnp.einsum("rf,fd->rd", d_gate_act, gate_w, preferred_element_type=jnp.float32)
        part = part + jnp.einsum("rf,fd->rd", d_up_act, up_w, preferred_element_type=jnp.float32)
        part = part.astype(jnp.bfloat16).reshape(2, 4, rows, features)
        return part, (x_rows, g_rows, hidden, d_gate_act, d_up_act)

    def near_of(mine, from_x, from_y, from_z):
        return jnp.concatenate([mine, from_x, from_y, from_z], axis=1)

    def far_of(second_x, second_y, second_z, third_x, third_y):
        return jnp.stack(
            [
                rows_of(second_y[0], second_y[1], second_z[0], third_y),
                rows_of(second_x[0], second_z[1], second_x[1], third_x),
            ]
        )

    def firsts(mine):
        return over_x(mine), over_y(mine), over_z(mine)

    def seconds(from_x, from_y, from_z):
        return (
            over_x(jnp.stack([from_y[1], from_z[1]])),
            over_y(jnp.stack([from_x[0], from_z[0]])),
            over_z(jnp.stack([from_x[0], from_y[1]])),
        )

    def thirds(second_z):
        return over_x(second_z[1]), over_y(second_z[0])

    scales = gate_of_expert(routes, gates, experts)
    scales = jnp.pad(scales, ((0, 0), (0, LANES - experts)))
    tail = ((0, 0), (0, LANES))
    grad_rows = jnp.concatenate([out_grad, scales], axis=1)
    mine = jnp.stack([jnp.pad(tokens, tail), grad_rows])
    from_x, from_y, from_z = firsts(mine)
    distant_t = over_far_z(tokens)
    mine, distant_t = together((mine, distant_t))
    distant_g = over_far_z(mine[1])
    from_x, from_y = together((from_x, from_y))
    g_far, t_far = over_x(from_y[1]), over_y(from_x[0])
    from_z, g_far, t_far = together((from_z, g_far, t_far))
    z_x, z_y = over_x(from_z), over_y(from_z)
    corner = over_z(jnp.stack([t_far, g_far]))
    near = near_of(mine, from_x, from_y, from_z)
    near_other = over_core(near)
    z_x, z_y, corner, near_other, distant_t, distant_g = together((z_x, z_y, corner, near_other, distant_t, distant_g))
    distant = jnp.stack([jnp.pad(distant_t, tail), distant_g])
    first2 = firsts(distant)
    part_near, kept_near = expert_rows(near, near_other)
    far = jnp.stack(
        [rows_of(t_far, z_y[0], z_x[0], corner[0]), rows_of(g_far, z_y[1], z_x[1], corner[1])]
    )
    far_other = over_core(far)
    first2, part_near, far_other = together((first2, part_near, far_other))
    part_far, kept_far = expert_rows(far, far_other)
    second2 = seconds(*first2)
    near2 = near_of(distant, *first2)
    near2_other = over_core(near2)
    part_far, kept_far = expert_rows(far, far_other)
    second2, near2_other, part_far = together((second2, near2_other, part_far))
    third2 = thirds(second2[2])
    others = over_core(part_near[1]), over_core(part_far[1])
    part_near2, kept_near2 = expert_rows(near2, near2_other)
    third2, others, part_near2 = together((third2, others, part_near2))
    far2 = far_of(*second2, *third2)
    far2_other = over_core(far2)

    def lane_sums(near_part, far_part, near_part_other, far_part_other):
        return tuple(summed(near_part[i], near_part_other[i]) for i in range(4)) + tuple(
            summed(far_part[i], far_part_other[i]) for i in range(4)
        )

    def opening_sends(sums):
        return over_x(sums[7][:, half:]), over_y(sums[7][:, :half])

    def middle_sends(sums):
        _, _, _, _, xy, yz, xz, _ = sums
        return over_x(jnp.stack([xy[:, half:], xz[:, half:]])), over_y(jnp.stack([xy[:, :half], yz[:, :half]]))

    def early_sends(sums):
        _, _, _, _, xy, yz, xz, xyz = sums
        in_x = over_x(jnp.stack([xyz[:, half:], xy[:, half:], xz[:, half:]]))
        in_y = over_y(jnp.stack([xyz[:, :half], xy[:, :half], yz[:, :half]]))
        return in_x, in_y

    def sent_z(sums, opening):
        _, _, _, _, _, yz, xz, _ = sums
        return over_z(jnp.concatenate([summed(xz[:, :half], opening[1]), summed(yz[:, half:], opening[0])], axis=1))

    def last_sends(sums, middle, from_z):
        _, x, y, z, _, _, _, _ = sums
        from_x, from_y = middle
        x = jnp.concatenate([summed(x[:, :half], from_y[0], from_z[:, :half]), x[:, half:]], axis=1)
        y = jnp.concatenate([y[:, :half], summed(y[:, half:], from_x[0], from_z[:, half:])], axis=1)
        z = jnp.concatenate([summed(z[:, :half], from_y[1]), summed(z[:, half:], from_x[1])], axis=1)
        return over_x(x), over_y(y), over_z(z)

    sums = lane_sums(part_near[0], part_far[0], *others)
    in_x, in_y = early_sends(sums)
    part_far2, kept_far2 = expert_rows(far2, far2_other)
    near2_back = over_core(part_near2[1])
    part_far2, in_x, in_y, near2_back = together((part_far2, in_x, in_y, near2_back))
    others2 = near2_back, over_core(part_far2[1])
    middle = in_x[1:], in_y[1:]
    from_z = sent_z(sums, (in_x[0], in_y[0]))
    sums2 = lane_sums(part_near2[0], part_far2[0], *others2)
    opening2, middle2 = opening_sends(sums2), middle_sends(sums2)
    from_z2 = sent_z(sums2, opening2)
    last2 = last_sends(sums2, middle2, from_z2)
    sums, middle, from_z, last2 = together((sums, middle, from_z, last2))
    returned = over_far_z(summed(sums2[0], *last2))
    last = last_sends(sums, middle, from_z)
    d_tokens = summed(sums[0], *last, returned)

    def weight_grad(at, side):
        kept = (kept_near, kept_far, kept_near2, kept_far2)
        return jnp.einsum(
            "rf,rd->fd",
            rows_of(*(held[at] for held in kept)),
            rows_of(*(held[side] for held in kept)),
            preferred_element_type=jnp.float32,
        ).astype(jnp.bfloat16)[None]

    return d_tokens, weight_grad(3, 0), weight_grad(4, 0), weight_grad(2, 1)


def per_device(tokens, out_grad, routes, gates, w_gate, w_up, w_down):
    tok_rows, top_count = routes.shape
    experts = lax.axis_size("expert")
    capacity = max(2, min(tok_rows, 3 * tok_rows * top_count // (2 * experts)))
    crowded = 2 * capacity >= tok_rows and lax.axis_size("dp") == 2 and experts == 16
    plan = dense_plan if crowded else slot_plan
    return plan(tokens, out_grad, routes, gates, w_gate, w_up, w_down)


def solution(mesh):
    in_specs = (
        P(("dp", "expert"), None),
        P(("dp", "expert"), None),
        P(("dp", "expert"), None),
        P(("dp", "expert"), None),
        P("expert", "dp", None),
        P("expert", "dp", None),
        P("expert", "dp", None),
    )
    out_specs = (
        P(("dp", "expert"), None),
        P("expert", "dp", None),
        P("expert", "dp", None),
        P("expert", "dp", None),
    )
    return jax.shard_map(
        per_device, mesh=mesh, in_specs=in_specs, out_specs=out_specs, check_vma=False
    )
```

```python
from functools import partial

import jax
import jax.numpy as jnp
from jax import lax
from jax.sharding import PartitionSpec as P


def cell_match(routes, experts, capacity):
    expert_ids = jnp.arange(experts, dtype=jnp.int32)
    onehot = (routes[:, :, None] == expert_ids).astype(jnp.int32)
    chosen = jnp.sum(onehot, axis=1)
    earlier = jnp.cumsum(chosen, axis=0) - chosen
    slot_index = jnp.sum(onehot * earlier[:, None, :], axis=2)
    target = routes * capacity + slot_index
    cell_ids = jnp.arange(experts * capacity, dtype=jnp.int32)
    return target[:, :, None] == cell_ids


def placement(matches, experts, capacity):
    return jnp.any(matches, axis=1).reshape(-1, experts, capacity).astype(jnp.bfloat16)


def weighting(matches, gates, experts, capacity):
    spread = jnp.where(matches, gates.astype(jnp.float32)[:, :, None], 0.0)
    return jnp.sum(spread, axis=1).reshape(-1, experts, capacity)


def slot_plan(tokens, out_grad, routes, gates, w_gate, w_up, w_down):
    tok_rows, features = tokens.shape
    top_count = routes.shape[1]
    experts = lax.axis_size("expert")
    groups = lax.axis_size("dp")
    capacity = max(2, min(tok_rows, 3 * tok_rows * top_count // (2 * experts)))
    match_fn = partial(cell_match, experts=experts, capacity=capacity)
    place_fn = partial(placement, experts=experts, capacity=capacity)
    weight_fn = partial(weighting, experts=experts, capacity=capacity)
    own_match = match_fn(routes)
    own_place = place_fn(own_match)
    own_weight = weight_fn(own_match, gates)
    input_send = jnp.einsum(
        "tec,td->ecd", own_place, tokens, preferred_element_type=jnp.float32
    ).astype(jnp.bfloat16)
    grad_send = jnp.einsum(
        "tec,td->ecd", own_weight, out_grad.astype(jnp.float32), precision=lax.Precision.HIGHEST
    ).astype(jnp.bfloat16)
    input_recv, grad_recv = (
        lax.all_to_all(input_send, "expert", split_axis=0, concat_axis=0, tiled=True),
        lax.all_to_all(grad_send, "expert", split_axis=0, concat_axis=0, tiled=True),
    )
    input_recv = input_recv.reshape(experts, 1, capacity, features)
    grad_recv = grad_recv.reshape(experts, 1, capacity, features)
    input_slots, grad_slots = (
        lax.all_gather(input_recv, "dp", axis=1, tiled=True),
        lax.all_gather(grad_recv, "dp", axis=1, tiled=True),
    )
    input_rows = input_slots.reshape(-1, features)
    grad_rows = grad_slots.reshape(-1, features)
    gate_w = w_gate[0]
    up_w = w_up[0]
    down_w = w_down[0]
    gate_pre = jnp.einsum("rd,fd->rf", input_rows, gate_w, preferred_element_type=jnp.float32)
    up_pre = jnp.einsum("rd,fd->rf", input_rows, up_w, preferred_element_type=jnp.float32)
    sigmoid_gate = jax.nn.sigmoid(gate_pre)
    silu_gate = gate_pre * sigmoid_gate
    hidden = (silu_gate * up_pre).astype(jnp.bfloat16)
    d_hidden = jnp.einsum("rd,fd->rf", grad_rows, down_w, preferred_element_type=jnp.float32)
    d_up_act = (d_hidden * silu_gate).astype(jnp.bfloat16)
    d_gate_act = (
        d_hidden * up_pre * sigmoid_gate * (1.0 + gate_pre * (1.0 - sigmoid_gate))
    ).astype(jnp.bfloat16)
    grad_down = jnp.einsum(
        "rf,rd->fd", hidden, grad_rows, preferred_element_type=jnp.float32
    ).astype(jnp.bfloat16)
    grad_gate = jnp.einsum(
        "rf,rd->fd", d_gate_act, input_rows, preferred_element_type=jnp.float32
    ).astype(jnp.bfloat16)
    grad_up = jnp.einsum(
        "rf,rd->fd", d_up_act, input_rows, preferred_element_type=jnp.float32
    ).astype(jnp.bfloat16)
    partial_sum = jnp.einsum("rf,fd->rd", d_gate_act, gate_w, preferred_element_type=jnp.float32)
    partial_sum = partial_sum + jnp.einsum(
        "rf,fd->rd", d_up_act, up_w, preferred_element_type=jnp.float32
    )
    rounded = partial_sum.astype(jnp.bfloat16).reshape(experts, groups, capacity, features)
    held = lax.optimization_barrier(rounded).astype(jnp.float32)
    slot_total = lax.psum_scatter(
        held.astype(jnp.bfloat16), "dp", scatter_dimension=1, tiled=True
    ).astype(jnp.float32)
    returned = lax.all_to_all(
        slot_total[:, 0].astype(jnp.bfloat16), "expert", split_axis=0, concat_axis=0, tiled=True
    ).astype(jnp.float32)
    summed = jnp.einsum(
        "tec,ecd->td", own_place.astype(jnp.float32), returned, precision=lax.Precision.HIGHEST
    )
    return (summed.astype(jnp.bfloat16), grad_gate[None], grad_up[None], grad_down[None])


def swapped(x, axis, bits):
    count = lax.axis_size(axis)
    return lax.ppermute(x, axis, [(i, i ^ bits) for i in range(count)])


over_core = partial(swapped, axis="expert", bits=1)
over_x = partial(swapped, axis="expert", bits=2)
over_z = partial(swapped, axis="expert", bits=4)
over_far_z = partial(swapped, axis="expert", bits=8)
over_y = partial(swapped, axis="dp", bits=1)
together = lax.optimization_barrier
LANES = 128


def gate_of_expert(routes, gates, experts):
    hit = routes[:, :, None] == jnp.arange(experts, dtype=jnp.int32)
    return jnp.sum(jnp.where(hit, gates[:, :, None], 0), axis=1).astype(jnp.bfloat16)


def summed(*terms):
    total = terms[0].astype(jnp.float32)
    for term in terms[1:]:
        total = total + term.astype(jnp.float32)
    return total.astype(jnp.bfloat16)


def rows_of(*pieces):
    return jnp.concatenate(pieces, axis=0)


def first_sends(part):
    half = part.shape[-1] // 2
    return part[..., :half], part[..., half:]


def dense_plan(tokens, out_grad, routes, gates, w_gate, w_up, w_down):
    rows, features = tokens.shape
    experts = lax.axis_size("expert")
    half = features // 2
    gate_w, up_w, down_w = w_gate[0], w_up[0], w_down[0]
    own = jnp.arange(LANES, dtype=jnp.int32) == lax.axis_index("expert")

    def expert_rows(lane, other):
        x_rows = rows_of(lane[0], other[0])[:, :features]
        g_rows = rows_of(lane[1], other[1])
        scale = g_rows[:, features:].astype(jnp.float32)
        scale = jnp.sum(jnp.where(own, scale, 0.0), axis=-1, keepdims=True)
        g_rows = g_rows[:, :features]
        gate_pre = jnp.einsum("rd,fd->rf", x_rows, gate_w, preferred_element_type=jnp.float32)
        up_pre = jnp.einsum("rd,fd->rf", x_rows, up_w, preferred_element_type=jnp.float32)
        d_hidden = scale * jnp.einsum("rd,fd->rf", g_rows, down_w, preferred_element_type=jnp.float32)
        sigmoid_gate = jax.nn.sigmoid(gate_pre)
        silu_gate = gate_pre * sigmoid_gate
        hidden = (scale * silu_gate * up_pre).astype(jnp.bfloat16)
        d_up_act = (d_hidden * silu_gate).astype(jnp.bfloat16)
        d_gate_act = (
            d_hidden * up_pre * sigmoid_gate * (1.0 + gate_pre * (1.0 - sigmoid_gate))
        ).astype(jnp.bfloat16)
        part = jnp.einsum("rf,fd->rd", d_gate_act, gate_w, preferred_element_type=jnp.float32)
        part = part + jnp.einsum("rf,fd->rd", d_up_act, up_w, preferred_element_type=jnp.float32)
        part = part.astype(jnp.bfloat16).reshape(2, 4, rows, features)
        return part, (x_rows, g_rows, hidden, d_gate_act, d_up_act)

    def near_of(mine, from_x, from_y, from_z):
        return jnp.concatenate([mine, from_x, from_y, from_z], axis=1)

    def far_of(second_x, second_y, second_z, third_x, third_y):
        return jnp.stack(
            [
                rows_of(second_y[0], second_y[1], second_z[0], third_y),
                rows_of(second_x[0], second_z[1], second_x[1], third_x),
            ]
        )

    def firsts(mine):
        return over_x(mine), over_y(mine), over_z(mine)

    def seconds(from_x, from_y, from_z):
        return (
            over_x(jnp.stack([from_y[1], from_z[1]])),
            over_y(jnp.stack([from_x[0], from_z[0]])),
            over_z(jnp.stack([from_x[0], from_y[1]])),
        )

    def thirds(second_z):
        return over_x(second_z[1]), over_y(second_z[0])

    scales = gate_of_expert(routes, gates, experts)
    scales = jnp.pad(scales, ((0, 0), (0, LANES - experts)))
    tail = ((0, 0), (0, LANES))
    grad_rows = jnp.concatenate([out_grad, scales], axis=1)
    mine = jnp.stack([jnp.pad(tokens, tail), grad_rows])
    from_x, from_y, from_z = firsts(mine)
    distant_t = over_far_z(tokens)
    mine, distant_t = together((mine, distant_t))
    distant_g = over_far_z(mine[1])
    from_x, from_y = together((from_x, from_y))
    g_far, t_far = over_x(from_y[1]), over_y(from_x[0])
    from_z, g_far, t_far = together((from_z, g_far, t_far))
    z_x, z_y = over_x(from_z), over_y(from_z)
    corner = over_z(jnp.stack([t_far, g_far]))
    near = near_of(mine, from_x, from_y, from_z)
    near_other = over_core(near)
    z_x, z_y, corner, near_other, distant_t, distant_g = together((z_x, z_y, corner, near_other, distant_t, distant_g))
    distant = jnp.stack([jnp.pad(distant_t, tail), distant_g])
    first2 = firsts(distant)
    part_near, kept_near = expert_rows(near, near_other)
    far = jnp.stack(
        [rows_of(t_far, z_y[0], z_x[0], corner[0]), rows_of(g_far, z_y[1], z_x[1], corner[1])]
    )
    far_other = over_core(far)
    first2, part_near, far_other = together((first2, part_near, far_other))
    part_far, kept_far = expert_rows(far, far_other)
    second2 = seconds(*first2)
    near2 = near_of(distant, *first2)
    near2_other = over_core(near2)
    part_far, kept_far = expert_rows(far, far_other)
    second2, part_far = together((second2, part_far))
    third2 = thirds(second2[2])
    others = over_core(part_near[1]), over_core(part_far[1])
    part_near2, kept_near2 = expert_rows(near2, near2_other)
    third2, others, part_near2 = together((third2, others, part_near2))
    far2 = far_of(*second2, *third2)
    far2_other = over_core(far2)

    def lane_sums(near_part, far_part, near_part_other, far_part_other):
        return tuple(summed(near_part[i], near_part_other[i]) for i in range(4)) + tuple(
            summed(far_part[i], far_part_other[i]) for i in range(4)
        )

    def opening_sends(sums):
        return over_x(sums[7][:, half:]), over_y(sums[7][:, :half])

    def middle_sends(sums):
        _, _, _, _, xy, yz, xz, _ = sums
        return over_x(jnp.stack([xy[:, half:], xz[:, half:]])), over_y(jnp.stack([xy[:, :half], yz[:, :half]]))

    def early_sends(sums):
        _, _, _, _, xy, yz, xz, xyz = sums
        in_x = over_x(jnp.stack([xyz[:, half:], xy[:, half:], xz[:, half:]]))
        in_y = over_y(jnp.stack([xyz[:, :half], xy[:, :half], yz[:, :half]]))
        return in_x, in_y

    def sent_z(sums, opening):
        _, _, _, _, _, yz, xz, _ = sums
        return over_z(jnp.concatenate([summed(xz[:, :half], opening[1]), summed(yz[:, half:], opening[0])], axis=1))

    def last_sends(sums, middle, from_z):
        _, x, y, z, _, _, _, _ = sums
        from_x, from_y = middle
        x = jnp.concatenate([summed(x[:, :half], from_y[0], from_z[:, :half]), x[:, half:]], axis=1)
        y = jnp.concatenate([y[:, :half], summed(y[:, half:], from_x[0], from_z[:, half:])], axis=1)
        z = jnp.concatenate([summed(z[:, :half], from_y[1]), summed(z[:, half:], from_x[1])], axis=1)
        return over_x(x), over_y(y), over_z(z)

    sums = lane_sums(part_near[0], part_far[0], *others)
    in_x, in_y = early_sends(sums)
    part_far2, kept_far2 = expert_rows(far2, far2_other)
    near2_back = over_core(part_near2[1])
    part_far2, in_x, in_y, near2_back = together((part_far2, in_x, in_y, near2_back))
    others2 = near2_back, over_core(part_far2[1])
    middle = in_x[1:], in_y[1:]
    from_z = sent_z(sums, (in_x[0], in_y[0]))
    sums2 = lane_sums(part_near2[0], part_far2[0], *others2)
    opening2, middle2 = opening_sends(sums2), middle_sends(sums2)
    from_z2 = sent_z(sums2, opening2)
    last2 = last_sends(sums2, middle2, from_z2)
    sums, middle, from_z, last2 = together((sums, middle, from_z, last2))
    returned = over_far_z(summed(sums2[0], *last2))
    last = last_sends(sums, middle, from_z)
    d_tokens = summed(sums[0], *last, returned)

    def weight_grad(at, side):
        kept = (kept_near, kept_far, kept_near2, kept_far2)
        return jnp.einsum(
            "rf,rd->fd",
            rows_of(*(held[at] for held in kept)),
            rows_of(*(held[side] for held in kept)),
            preferred_element_type=jnp.float32,
        ).astype(jnp.bfloat16)[None]

    return d_tokens, weight_grad(3, 0), weight_grad(4, 0), weight_grad(2, 1)


def per_device(tokens, out_grad, routes, gates, w_gate, w_up, w_down):
    tok_rows, top_count = routes.shape
    experts = lax.axis_size("expert")
    capacity = max(2, min(tok_rows, 3 * tok_rows * top_count // (2 * experts)))
    crowded = 2 * capacity >= tok_rows and lax.axis_size("dp") == 2 and experts == 16
    plan = dense_plan if crowded else slot_plan
    return plan(tokens, out_grad, routes, gates, w_gate, w_up, w_down)


def solution(mesh):
    in_specs = (
        P(("dp", "expert"), None),
        P(("dp", "expert"), None),
        P(("dp", "expert"), None),
        P(("dp", "expert"), None),
        P("expert", "dp", None),
        P("expert", "dp", None),
        P("expert", "dp", None),
    )
    out_specs = (
        P(("dp", "expert"), None),
        P("expert", "dp", None),
        P("expert", "dp", None),
        P("expert", "dp", None),
    )
    return jax.shard_map(
        per_device, mesh=mesh, in_specs=in_specs, out_specs=out_specs, check_vma=False
    )
```
